32 devices in a mesh: shard: 8 (over y, x, core), rep: 4 (over z).
Axes of the slice: x: 2, y: 2, z: 4, core: 2. Of those that a mesh axis runs over, the one named last changes fastest.
Arguments:
- rows_in: bfloat16 [16384, 2048], P(('shard', 'rep')), may hold values from -6 to 6
- cotangent: bfloat16 [16384, 2048], P(('shard', 'rep')), may hold values from -6 to 6
- expert_counts: int32 [32, 2], P(('shard', 'rep')), may hold values from 0 to 512, as said below
- weights: bfloat16 [2048, 2, 1152], P('shard'), may hold values from -0.125 to 0.125
Outputs:
- rows_out: bfloat16 [16384, 2048], P(('shard', 'rep'))
- rows_grad: bfloat16 [16384, 2048], P(('shard', 'rep'))
- weight_grad: float32 [2048, 2, 1152], P('shard')
The draws below stay inside these ranges and needn't reach their ends.
Inputs may be any that keep to these rules, and one draw needn't show every extreme that they name: `expert_counts`: on each device the experts' regions, each padded to a multiple of 128 rows, follow one another from row 0 and together fill at most 512 rows; some device fills all 512; one expert on some device holds all 512 rows.
All inputs are finite; a program needn't handle non-finite values.
Results may differ from the reference program's by a relative error of at most 0.0095.
Values may be sent and summed in bfloat16 or wider, within the bound.
A program may use at most 128 MiB of HBM per device.

```python
import jax
import jax.numpy as jnp
from jax import lax

D = 2048
FF = 384
G = 2
BLOCK = 128
ROWS_DEV = 512
NDEV = 32
ROWS = 16384


def draw_expert_counts(key, part):
    nblocks = ROWS_DEV // BLOCK
    key_total, key_full, key_first, key_tail = jax.random.split(key, 4)
    totals = jax.random.randint(key_total, (NDEV,), 1, nblocks + 1)
    fuller = jax.random.randint(key_full, (), 0, NDEV)
    is_fuller = jnp.arange(NDEV) == fuller
    totals = jnp.where(is_fuller, nblocks, totals)
    firsts = jax.random.randint(key_first, (NDEV,), 0, totals + 1)
    firsts = jnp.where(is_fuller, nblocks, firsts)
    blocks = jnp.stack([firsts, totals - firsts], axis=1)
    tails = jax.random.randint(key_tail, (NDEV, G), 1, BLOCK + 1)
    tails = jnp.where(is_fuller[:, None], BLOCK, tails)
    counts = jnp.where(blocks > 0, (blocks - 1) * BLOCK + tails, 0)
    return counts.astype(jnp.int32)


def raised(result, key, source, target, shards_of, factor):
    owner, partner = [(jnp.arange(result.shape[axis_at]) // (result.shape[axis_at] // shards_of)).reshape([-1 if axis == axis_at else 1 for axis in range(result.ndim)]) for axis_at in (source, target)]
    chosen = jax.random.permutation(key, shards_of)[partner]
    strong = (owner == chosen) | (owner == (partner + shards_of // 2) % shards_of)
    return jnp.where(strong, factor * result, result)


def block_levels(rng, shape, pieces, low, top_value):
    factor_of, own = 1.0, jax.random.fold_in(rng, 6)
    for dim, parts in pieces:
        draws = jnp.exp(jax.random.uniform(jax.random.fold_in(own, dim), (parts,), jnp.float32, low / len(pieces), top_value / len(pieces)))
        factor_of = factor_of * jnp.repeat(draws, shape[dim] // parts).reshape([-1 if axis == dim else 1 for axis in range(len(shape))])
    return factor_of


def scatter_about(key, shape, width, reach, shards=(), kind=jnp.bfloat16):
    values = jax.random.normal(key, shape, jnp.float32) * width
    if len(shards) > 0:
        values = block_levels(key, shape, shards, -0.22, 0.18) * values
    return jnp.clip(values, min=-reach, max=reach).astype(kind)


def heavy_noise(stream_key, extent, scale, most, pieces, heavy, kind=jnp.bfloat16):
    entries = scale * jax.random.normal(stream_key, extent, jnp.float32)
    if pieces:
        entries = entries * block_levels(stream_key, extent, pieces, -0.22, 0.18)
    return jnp.clip(raised(entries, jax.random.fold_in(stream_key, 3), *heavy), -most, most).astype(kind)


def setup_inputs(seed: int = 0) -> dict:
    splits = jax.random.split(jax.random.key(seed), 5)
    return {
        "rows_in": heavy_noise(splits[0], (ROWS, D), 1.0, 6.0, ((0, 32),), (0, 1, 32, 2.75)),
        "cotangent": heavy_noise(splits[1], (ROWS, D), 1.0, 6.0, ((0, 32),), (0, 1, 32, 2.75)),
        "expert_counts": draw_expert_counts(jax.random.fold_in(splits[4], 71), 0),
        "weights": scatter_about(splits[3], (D, G, 3 * FF), D ** -0.5, 0.125, ((0, 8),)),
    }


def expert_block(inputs, upstream, expert_slab):
    hidden_width = expert_slab.shape[1] // 3
    gate_up = expert_slab[:, :2 * hidden_width]
    down_t = expert_slab[:, 2 * hidden_width:]
    project = jnp.dot(inputs, gate_up, preferred_element_type=jnp.float32)
    gate_pre = project[:, :hidden_width]
    up_pre = project[:, hidden_width:]
    gate_sigmoid = jax.nn.sigmoid(gate_pre)
    active = gate_pre * gate_sigmoid
    hidden = (active * up_pre).astype(jnp.bfloat16)
    output = lax.dot_general(hidden, down_t, (((1,), (1,)), ((), ())), preferred_element_type=jnp.float32).astype(jnp.bfloat16)
    hidden_grad = jnp.dot(upstream, down_t, preferred_element_type=jnp.float32)
    down_grad = lax.dot_general(upstream, hidden, (((0,), (0,)), ((), ())), preferred_element_type=jnp.float32)
    gate_grad = hidden_grad * up_pre * gate_sigmoid * (1.0 + gate_pre * (1.0 - gate_sigmoid))
    up_grad = hidden_grad * active
    joint_grad = jnp.concatenate([gate_grad, up_grad], axis=1).astype(jnp.bfloat16)
    proj_grad = lax.dot_general(inputs, joint_grad, (((0,), (0,)), ((), ())), preferred_element_type=jnp.float32)
    input_grad = lax.dot_general(joint_grad, gate_up, (((1,), (1,)), ((), ())), preferred_element_type=jnp.float32).astype(jnp.bfloat16)
    return output, input_grad, jnp.concatenate([proj_grad, down_grad], axis=1)


def alive_rows(counts, total_rows):
    padded = (counts + BLOCK - 1) // BLOCK * BLOCK
    starts = jnp.cumsum(padded) - padded
    position = jnp.arange(total_rows, dtype=jnp.int32)
    inside = (position[:, None] >= starts[None, :]) & (position[:, None] < (starts + counts)[None, :])
    return jnp.any(inside, axis=1), padded, starts


def reference(rows_in, cotangent, expert_counts, weights):
    def device_pass(grad_carry, device_items):
        inputs, upstream, counts = device_items
        alive, padded, starts = alive_rows(counts, ROWS_DEV)
        inputs = jnp.where(alive[:, None], inputs, jnp.zeros_like(inputs))
        upstream = jnp.where(alive[:, None], upstream, jnp.zeros_like(upstream))

        def block_pass(grad_total, block_index):
            row_begin = (block_index * BLOCK).astype(jnp.int32)
            owner_index = (jnp.sum((starts <= row_begin).astype(jnp.int32)) - 1).astype(jnp.int32)
            expert_slab = lax.dynamic_index_in_dim(weights, owner_index, 1, keepdims=False)
            block_in = lax.dynamic_slice_in_dim(inputs, row_begin, BLOCK, 0)
            block_up = lax.dynamic_slice_in_dim(upstream, row_begin, BLOCK, 0)
            output, input_grad, grad_piece = expert_block(block_in, block_up, expert_slab)
            current = lax.dynamic_index_in_dim(grad_total, owner_index, 1, keepdims=False)
            grad_total = lax.dynamic_update_index_in_dim(grad_total, current + grad_piece, owner_index, 1)
            return grad_total, (output, input_grad)

        grad_carry, (outputs, input_grads) = lax.scan(block_pass, grad_carry, jnp.arange(ROWS_DEV // BLOCK, dtype=jnp.int32))
        return grad_carry, (outputs.reshape(ROWS_DEV, D), input_grads.reshape(ROWS_DEV, D))

    start_grad = jnp.zeros((D, G, 3 * FF), jnp.float32)
    device_rows = rows_in.reshape(NDEV, ROWS_DEV, D)
    device_cots = cotangent.reshape(NDEV, ROWS_DEV, D)
    weight_grad, (rows_out, rows_grad) = lax.scan(device_pass, start_grad, (device_rows, device_cots, expert_counts))
    return rows_out.reshape(ROWS, D), rows_grad.reshape(ROWS, D), weight_grad
```

```python
import functools

import jax
import jax.numpy as jnp
from jax import lax
from jax.experimental import pallas as pl
from jax.experimental.pallas import tpu as pltpu
from jax.sharding import PartitionSpec as P

BLOCK = 128
INNER = 8
MESH = pl.DeviceIdType.MESH
BF16, F32 = jnp.bfloat16, jnp.float32


def flip(index, bit):
    return index + bit - 2 * bit * lax.rem(lax.div(index, bit), 2)


def dot(a, b, dims):
    return lax.dot_general(a, b, (dims, ((), ())), preferred_element_type=F32)


NN, NT, TN = ((1,), (0,)), ((1,), (1,)), ((0,), (0,))


def kernel(
    counts_ref, x_ref, dy_ref, w_ref,
    out_ref, grad_ref, wg_ref,
    w_all, pre, hgrad, hid, joint,
    core_out, core_in, first_out, first_in, second_out, second_in, acc,
    z_out, z_in, z_peer, z_fin,
    w_sem, ag_send, ag_recv, core_send, core_recv, xy_send, xy_recv, z_send, z_recv,
):
    rows = x_ref.shape[0]
    experts, feat, width = w_ref.shape
    ff = width // 3
    shard = lax.axis_index("shard")
    rep = lax.axis_index("rep")
    local = lax.rem(shard, INNER)
    to_core, to_x, to_y = ((flip(shard, b), rep) for b in (1, 2, 4))
    z_pair, z_mirror = (shard, flip(rep, 1)), (shard, 3 - rep)
    inner_z = jnp.logical_or(rep == 1, rep == 2)
    partner = flip(local, 1)
    near = [local, flip(local, 2), flip(local, 4), flip(flip(local, 2), 4)]
    far = [partner, flip(partner, 2), flip(partner, 4), flip(flip(partner, 2), 4)]

    load = pltpu.make_async_copy(w_ref, w_all.at[local], w_sem)
    load.start()
    barrier = pltpu.get_barrier_semaphore()
    for other in (to_core, to_x, to_y, z_pair, z_mirror):
        pl.semaphore_signal(barrier, inc=1, device_id=other, device_id_type=MESH)
    load.wait()
    pl.semaphore_wait(barrier, 5)

    def share(k, member, e, device):
        block = w_all.at[member, e]
        return pltpu.make_async_remote_copy(
            src_ref=block, dst_ref=block, send_sem=ag_send.at[k], recv_sem=ag_recv.at[k],
            device_id=device, device_id_type=MESH,
        )

    gather = [
        share(0, near[0], 0, to_x), share(1, near[0], 1, to_x),
        share(2, near[0], 0, to_y), share(3, near[0], 1, to_y),
        share(4, near[1], 0, to_y), share(5, near[2], 1, to_x),
    ] + [share(6 + 2 * d + e, near[d], e, to_core) for d in range(4) for e in range(2)]
    for k in (0, 3, 6, 7, 1, 2):
        gather[k].start()

    position = lax.broadcasted_iota(jnp.int32, (rows, 1), 0)
    masks, start = [], jnp.int32(0)
    for e in range(experts):
        count = counts_ref[0, e]
        masks.append((position >= start) & (position < start + count))
        start = start + lax.div(count + (BLOCK - 1), BLOCK) * BLOCK

    def columns(member):
        return pl.ds(pl.multiple_of(member * feat, 128), feat)

    def project(member, first=False):
        x = x_ref[:, columns(member)]
        dy = dy_ref[:, columns(member)]
        zero = jnp.zeros_like(x)
        xs = [jnp.where(m, x, zero) for m in masks]
        dys = [jnp.where(m, dy, zero) for m in masks]
        p = sum(dot(xs[e], w_all[member, e, :, : 2 * ff], NN) for e in range(experts))
        h = sum(dot(dys[e], w_all[member, e, :, 2 * ff :], NN) for e in range(experts))
        if first:
            pre[...] = p
            hgrad[...] = h
        else:
            pre[...] += p
            hgrad[...] += h

    project(near[0], True)
    gather[6].wait_recv()
    gather[7].wait_recv()
    project(far[0])
    gather[0].wait_recv()
    gather[4].start()
    gather[8].start()
    gather[3].wait_recv()
    gather[5].start()
    gather[11].start()
    gather[1].wait_recv()
    gather[9].start()
    gather[2].wait_recv()
    gather[10].start()
    project(near[1])
    project(near[2])
    gather[8].wait_recv()
    gather[9].wait_recv()
    project(far[1])
    gather[10].wait_recv()
    gather[11].wait_recv()
    project(far[2])
    gather[4].wait_recv()
    gather[12].start()
    gather[5].wait_recv()
    gather[13].start()
    project(near[3])
    gather[12].wait_recv()
    gather[13].wait_recv()
    project(far[3])

    def activate(i, carry):
        at = pl.ds(pl.multiple_of(i * BLOCK, BLOCK), BLOCK)
        a, b, g = pre[at, :ff], pre[at, ff:], hgrad[at, :]
        s = jax.nn.sigmoid(a)
        active = a * s
        hidden = (active * b).astype(BF16)
        ga = (g * b * s * (1.0 + a * (1.0 - s))).astype(BF16)
        gb = (g * active).astype(BF16)
        place = lax.broadcasted_iota(jnp.int32, (BLOCK, 1), 0) + i * BLOCK
        begin = jnp.int32(0)
        for e in range(experts):
            count = counts_ref[0, e]
            keep = (place >= begin) & (place < begin + count)
            begin = begin + lax.div(count + (BLOCK - 1), BLOCK) * BLOCK
            zero = jnp.zeros_like(hidden)
            hid[e, at, :] = jnp.where(keep, hidden, zero)
            joint[e, at, :ff] = jnp.where(keep, ga, zero)
            joint[e, at, ff:] = jnp.where(keep, gb, zero)
        return carry

    lax.fori_loop(0, rows // BLOCK, activate, 0)

    def terms(member, e):
        at = columns(member)
        return (
            (slice(0, 2 * ff), dot(x_ref[:, at], joint[e], TN)),
            (slice(2 * ff, width), dot(dy_ref[:, at], hid[e], TN)),
        )

    def swap(d, e):
        return pltpu.make_async_remote_copy(
            src_ref=core_out.at[d, e], dst_ref=core_in.at[d, e],
            send_sem=core_send.at[d, e], recv_sem=core_recv.at[d, e],
            device_id=to_core, device_id_type=MESH,
        )

    def to_partner(d, e):
        for cols, value in terms(far[d], e):
            core_out[d, e, :, cols] = value.astype(BF16)
        swap(d, e).start()

    def step(k, src, dst, device):
        return pltpu.make_async_remote_copy(
            src_ref=src, dst_ref=dst, send_sem=xy_send.at[k], recv_sem=xy_recv.at[k],
            device_id=device, device_id_type=MESH,
        )

    first = [step(k, first_out.at[k], first_in.at[k], (to_x, to_y)[k % 2]) for k in range(4)]
    second = [step(4 + k, second_out.at[k], second_in.at[k], (to_y, to_x)[k]) for k in range(2)]

    def send_first(k, d, e):
        swap(d, e).wait_recv()
        for cols, value in terms(near[d], e):
            first_out[k, :, cols] = (value + core_in[d, e, :, cols].astype(F32)).astype(BF16)
        first[k].start()

    def keep_sum(k, d, e):
        swap(d, e).wait_recv()
        for cols, value in terms(near[d], e):
            acc[k, :, cols] = value + core_in[d, e, :, cols].astype(F32)

    def rows_of(member, carry):
        at = columns(member)
        out_ref[:, at] = sum(
            dot(hid[e], w_all[member, e, :, 2 * ff :], NT) for e in range(experts)
        ).astype(BF16)
        grad_ref[:, at] = sum(
            dot(joint[e], w_all[member, e, :, : 2 * ff], NT) for e in range(experts)
        ).astype(BF16)
        return carry

    to_partner(3, 0)
    to_partner(3, 1)
    send_first(0, 3, 0)
    send_first(1, 3, 1)
    to_partner(1, 0)
    to_partner(2, 1)
    send_first(2, 1, 0)
    send_first(3, 2, 1)
    to_partner(2, 0)
    to_partner(1, 1)
    to_partner(0, 0)
    to_partner(0, 1)
    keep_sum(0, 2, 0)
    keep_sum(1, 1, 1)
    keep_sum(2, 0, 0)
    keep_sum(3, 0, 1)
    for k in range(2):
        first[k].wait_recv()
        second_out[k] = (acc[k] + first_in[k].astype(F32)).astype(BF16)
        second[k].start()
    lax.fori_loop(0, INNER, rows_of, 0)
    for k in range(2):
        first[2 + k].wait_recv()
        acc[2 + k] += first_in[2 + k].astype(F32)

    def hop(j, k, src, dst, device):
        return pltpu.make_async_remote_copy(
            src_ref=src, dst_ref=dst, send_sem=z_send.at[j, k], recv_sem=z_recv.at[j, k],
            device_id=device, device_id_type=MESH,
        )

    half = feat // 2
    pieces = 2 * experts
    inward = [hop(0, k, z_out.at[k], z_in.at[k], z_pair) for k in range(pieces)]
    across = [hop(1, k, z_out.at[k], z_peer.at[k], z_mirror) for k in range(pieces)]
    outward = [hop(2, k, z_fin.at[k], z_fin.at[k], z_pair) for k in range(pieces)]

    for k in range(pieces):
        e, part = k // 2, slice((k % 2) * half, (k % 2 + 1) * half)
        if k % 2 == 0:
            second[e].wait_recv()

        @pl.when(jnp.logical_not(inner_z))
        def _():
            z_out[k] = (acc[2 + e, part] + second_in[e, part].astype(F32)).astype(BF16)
            inward[k].start()

        @pl.when(inner_z)
        def _():
            acc[2 + e, part] += second_in[e, part].astype(F32)

    @pl.when(inner_z)
    def _():
        for k in range(pieces):
            e, part = k // 2, slice((k % 2) * half, (k % 2 + 1) * half)
            inward[k].wait_recv()
            z_out[k] = (acc[2 + e, part] + z_in[k].astype(F32)).astype(BF16)
            across[k].start()
        for k in range(pieces):
            e, part = k // 2, slice((k % 2) * half, (k % 2 + 1) * half)
            across[k].wait_recv()
            z_fin[k] = (z_out[k].astype(F32) + z_peer[k].astype(F32)).astype(BF16)
            outward[k].start()
            wg_ref[e, part] = z_fin[k].astype(F32)
        for k in range(pieces):
            across[k].wait_send()
            outward[k].wait_send()

    @pl.when(jnp.logical_not(inner_z))
    def _():
        for k in range(pieces):
            e, part = k // 2, slice((k % 2) * half, (k % 2 + 1) * half)
            outward[k].wait_recv()
            wg_ref[e, part] = z_fin[k].astype(F32)
        for k in range(pieces):
            inward[k].wait_send()

    for copy in gather + first + second + [swap(d, e) for d in range(4) for e in range(experts)]:
        copy.wait_send()


def local(spread, rows_in, cotangent, expert_counts, weights):
    rows, model = rows_in.shape
    own, experts, width = weights.shape
    ff = width // 3
    feat = own * spread

    def regroup(v, a, b):
        return v if spread == 1 else v.reshape(rows, a, b, own).swapaxes(1, 2).reshape(rows, model)

    w = weights.swapaxes(0, 1)
    if spread > 1:
        peers = [[h * INNER + m for h in range(spread)] for m in range(INNER)]
        w = lax.all_gather(w, "shard", axis=1, tiled=True, axis_index_groups=peers)

    vmem = pl.BlockSpec(memory_space=pltpu.VMEM)
    dma = pltpu.SemaphoreType.DMA
    block = (feat, width)
    rows_out, rows_grad, wg = pl.pallas_call(
        kernel,
        out_shape=(
            jax.ShapeDtypeStruct((rows, model), BF16),
            jax.ShapeDtypeStruct((rows, model), BF16),
            jax.ShapeDtypeStruct((experts, feat, width), F32),
        ),
        in_specs=[
            pl.BlockSpec(memory_space=pltpu.SMEM), vmem, vmem,
            pl.BlockSpec(memory_space=pl.ANY),
        ],
        out_specs=(vmem, vmem, vmem),
        scratch_shapes=[
            pltpu.VMEM((INNER, experts, *block), BF16),
            pltpu.VMEM((rows, 2 * ff), F32),
            pltpu.VMEM((rows, ff), F32),
            pltpu.VMEM((experts, rows, ff), BF16),
            pltpu.VMEM((experts, rows, 2 * ff), BF16),
            pltpu.VMEM((4, experts, *block), BF16),
            pltpu.VMEM((4, experts, *block), BF16),
            pltpu.VMEM((4, *block), BF16),
            pltpu.VMEM((4, *block), BF16),
            pltpu.VMEM((2, *block), BF16),
            pltpu.VMEM((2, *block), BF16),
            pltpu.VMEM((4, *block), F32),
            pltpu.VMEM((2 * experts, feat // 2, width), BF16),
            pltpu.VMEM((2 * experts, feat // 2, width), BF16),
            pltpu.VMEM((2 * experts, feat // 2, width), BF16),
            pltpu.VMEM((2 * experts, feat // 2, width), BF16),
            dma,
            dma((14,)), dma((14,)),
            dma((4, experts)), dma((4, experts)),
            dma((6,)), dma((6,)),
            dma((3, 2 * experts)), dma((3, 2 * experts)),
        ],
        compiler_params=pltpu.CompilerParams(
            collective_id=0, has_side_effects=True, vmem_limit_bytes=62 * 1024 * 1024 - 1024 * 1024
        ),
        cost_estimate=pl.CostEstimate(
            flops=12 * rows * model * experts * width // 3 * 3, bytes_accessed=32 << 20,
            transcendentals=rows * ff,
        ),
    )(expert_counts, regroup(rows_in, spread, INNER), regroup(cotangent, spread, INNER), w)
    if spread > 1:
        wg = lax.psum_scatter(
            wg, "shard", scatter_dimension=1, tiled=True, axis_index_groups=peers
        )
    return regroup(rows_out, INNER, spread), regroup(rows_grad, INNER, spread), wg.swapaxes(0, 1)


def solution(mesh):
    rows_spec = P(("shard", "rep"), None)
    weight_spec = P("shard", None, None)
    return jax.shard_map(
        functools.partial(local, mesh.shape["shard"] // INNER),
        mesh=mesh,
        in_specs=(rows_spec, rows_spec, rows_spec, weight_spec),
        out_specs=(rows_spec, rows_spec, weight_spec),
        check_vma=False,
    )
```

```python
import functools

import jax
import jax.numpy as jnp
from jax import lax
from jax.experimental import pallas as pl
from jax.experimental.pallas import tpu as pltpu
from jax.sharding import PartitionSpec as P

BLOCK = 128
INNER = 8
MESH = pl.DeviceIdType.MESH
BF16, F32 = jnp.bfloat16, jnp.float32


def flip(index, bit):
    return index + bit - 2 * bit * lax.rem(lax.div(index, bit), 2)


def dot(a, b, dims):
    return lax.dot_general(a, b, (dims, ((), ())), preferred_element_type=F32)


NN, NT, TN = ((1,), (0,)), ((1,), (1,)), ((0,), (0,))


def kernel(
    counts_ref, x_ref, dy_ref, w_ref,
    out_ref, grad_ref, wg_ref,
    w_all, pre, hgrad, ops,
    core_out, core_in, first_out, first_in, second_out, second_in, acc,
    z_out, z_in, z_peer, z_fin,
    w_sem, ag_send, ag_recv, core_send, core_recv, xy_send, xy_recv, z_send, z_recv,
):
    rows = x_ref.shape[0]
    experts, feat, width = w_ref.shape
    ff = width // 3
    shard = lax.axis_index("shard")
    rep = lax.axis_index("rep")
    local = lax.rem(shard, INNER)
    to_core, to_x, to_y = ((flip(shard, b), rep) for b in (1, 2, 4))
    z_pair, z_mirror = (shard, flip(rep, 1)), (shard, 3 - rep)
    inner_z = jnp.logical_or(rep == 1, rep == 2)
    partner = flip(local, 1)
    near = [local, flip(local, 2), flip(local, 4), flip(flip(local, 2), 4)]
    far = [partner, flip(partner, 2), flip(partner, 4), flip(flip(partner, 2), 4)]

    load = pltpu.make_async_copy(w_ref, w_all.at[local], w_sem)
    load.start()
    barrier = pltpu.get_barrier_semaphore()
    for other in (to_core, to_x, to_y, z_pair, z_mirror):
        pl.semaphore_signal(barrier, inc=1, device_id=other, device_id_type=MESH)
    load.wait()
    pl.semaphore_wait(barrier, 5)

    ex = lax.rem(rep, 2)
    ey = 1 - ex

    def share(k, member, e, device):
        block = w_all.at[member, e]
        return pltpu.make_async_remote_copy(
            src_ref=block, dst_ref=block, send_sem=ag_send.at[k], recv_sem=ag_recv.at[k],
            device_id=device, device_id_type=MESH,
        )

    over_x, over_y = share(0, near[0], ex, to_x), share(1, near[0], ey, to_y)
    on_y, on_x = share(2, near[1], ex, to_y), share(3, near[2], ey, to_x)
    pair_x, pair_y = share(4, near[1], ex, z_pair), share(5, near[2], ey, z_pair)
    held = [
        (0, 0), (0, 1), (1, ex), (2, ey), (1, ey), (2, ex), (3, ex), (3, ey),
    ]
    cross = [share(6 + k, near[d], e, to_core) for k, (d, e) in enumerate(held)]
    over_x.start()
    over_y.start()
    cross[0].start()
    cross[1].start()

    def span(e):
        padded = lax.div(counts_ref[0, 0] + (BLOCK - 1), BLOCK) * BLOCK
        begin = e * padded
        return begin, begin + counts_ref[0, e]

    def columns(member):
        return pl.ds(pl.multiple_of(member * feat, 128), feat)

    def project(member, e, first=False):
        position = lax.broadcasted_iota(jnp.int32, (rows, 1), 0)
        begin, end = span(e)
        keep = (position >= begin) & (position < end)
        x = x_ref[:, columns(member)]
        dy = dy_ref[:, columns(member)]
        zero = jnp.zeros_like(x)
        p = dot(jnp.where(keep, x, zero), w_all[member, e, :, : 2 * ff], NN)
        h = dot(jnp.where(keep, dy, zero), w_all[member, e, :, 2 * ff :], NN)
        if first:
            pre[...] = p
            hgrad[...] = h
        else:
            pre[...] += p
            hgrad[...] += h

    project(near[0], 0, True)
    project(near[0], 1)
    cross[0].wait_recv()
    cross[1].wait_recv()
    project(far[0], 0)
    project(far[0], 1)
    over_x.wait_recv()
    on_y.start()
    pair_x.start()
    cross[2].start()
    over_y.wait_recv()
    on_x.start()
    pair_y.start()
    cross[3].start()
    project(near[1], ex)
    project(near[2], ey)
    cross[2].wait_recv()
    project(far[1], ex)
    cross[3].wait_recv()
    project(far[2], ey)
    for k, copy in ((4, pair_x), (5, pair_y), (6, on_y), (7, on_x)):
        copy.wait_recv()
        cross[k].start()
    for d, e in held[4:]:
        project(near[d], e)
    for k in range(4, 8):
        cross[k].wait_recv()
        project(far[held[k][0]], held[k][1])

    def activate(i, carry):
        at = pl.ds(pl.multiple_of(i * BLOCK, BLOCK), BLOCK)
        a, b, g = pre[at, :ff], pre[at, ff:], hgrad[at, :]
        s = jax.nn.sigmoid(a)
        active = a * s
        values = (
            (g * b * s * (1.0 + a * (1.0 - s))).astype(BF16),
            (g * active).astype(BF16),
            (active * b).astype(BF16),
        )
        place = lax.broadcasted_iota(jnp.int32, (BLOCK, 1), 0) + i * BLOCK
        for e in range(experts):
            begin, end = span(e)
            keep = (place >= begin) & (place < end)
            for part, value in enumerate(values):
                ops[part, at, e * ff : (e + 1) * ff] = jnp.where(
                    keep, value, jnp.zeros_like(value)
                )
        return carry

    lax.fori_loop(0, rows // BLOCK, activate, 0)

    parts = 3

    def terms(member, part):
        source = dy_ref if part == 2 else x_ref
        return dot(source[:, columns(member)], ops[part], TN)

    def swap(part, d):
        return pltpu.make_async_remote_copy(
            src_ref=core_out.at[part, d], dst_ref=core_in.at[part, d],
            send_sem=core_send.at[part, d], recv_sem=core_recv.at[part, d],
            device_id=to_core, device_id_type=MESH,
        )

    def to_partner(part, d):
        core_out[part, d] = terms(far[d], part).astype(BF16)
        swap(part, d).start()

    def own_terms(part, d):
        value = terms(near[d], part)
        swap(part, d).wait_recv()
        value = value + core_in[part, d].astype(F32)
        return value[:, :ff], value[:, ff:]

    def step(part, k, src, dst, device):
        return pltpu.make_async_remote_copy(
            src_ref=src, dst_ref=dst, send_sem=xy_send.at[part, k], recv_sem=xy_recv.at[part, k],
            device_id=device, device_id_type=MESH,
        )

    first = [
        [step(p, k, first_out.at[p, k], first_in.at[p, k], (to_x, to_y)[k % 2]) for k in range(4)]
        for p in range(parts)
    ]
    second = [
        [step(p, 4 + k, second_out.at[p, k], second_in.at[p, k], (to_y, to_x)[k]) for k in range(2)]
        for p in range(parts)
    ]

    def send_first(part, k, value):
        first_out[part, k] = value.astype(BF16)
        first[part][k].start()

    def begin(part):
        to_partner(part, 3)
        to_partner(part, 1)
        zero, one = own_terms(part, 3)
        send_first(part, 0, zero)
        send_first(part, 1, one)
        to_partner(part, 2)
        zero, one = own_terms(part, 1)
        send_first(part, 2, zero)
        acc[part, 1] = one
        to_partner(part, 0)
        zero, one = own_terms(part, 2)
        send_first(part, 3, one)
        acc[part, 0] = zero
        zero, one = own_terms(part, 0)
        acc[part, 2] = zero
        acc[part, 3] = one

    def turn(part):
        for k in range(2):
            first[part][k].wait_recv()
            second_out[part, k] = (acc[part, k] + first_in[part, k].astype(F32)).astype(BF16)
            second[part][k].start()

    def hop(j, part, e, src, dst, device):
        return pltpu.make_async_remote_copy(
            src_ref=src.at[part, e], dst_ref=dst.at[part, e],
            send_sem=z_send.at[j, part, e], recv_sem=z_recv.at[j, part, e],
            device_id=device, device_id_type=MESH,
        )

    pieces = [(p, e) for p in range(parts) for e in range(experts)]
    inward = {k: hop(0, *k, z_out, z_in, z_pair) for k in pieces}
    across = {k: hop(1, *k, z_out, z_peer, z_mirror) for k in pieces}
    outward = {k: hop(2, *k, z_fin, z_fin, z_pair) for k in pieces}

    def enter(part):
        for e in range(experts):
            first[part][2 + e].wait_recv()
            second[part][e].wait_recv()
            total = (
                acc[part, 2 + e]
                + first_in[part, 2 + e].astype(F32)
                + second_in[part, e].astype(F32)
            )

            @pl.when(jnp.logical_not(inner_z))
            def _():
                z_out[part, e] = total.astype(BF16)
                inward[part, e].start()

            @pl.when(inner_z)
            def _():
                acc[part, 2 + e] = total

    def meet(part):
        @pl.when(inner_z)
        def _():
            for e in range(experts):
                inward[part, e].wait_recv()
                z_out[part, e] = (acc[part, 2 + e] + z_in[part, e].astype(F32)).astype(BF16)
                across[part, e].start()

    def leave(part):
        @pl.when(inner_z)
        def _():
            for e in range(experts):
                across[part, e].wait_recv()
                z_fin[part, e] = (
                    z_out[part, e].astype(F32) + z_peer[part, e].astype(F32)
                ).astype(BF16)
                outward[part, e].start()
                wg_ref[e, :, part * ff : (part + 1) * ff] = z_fin[part, e].astype(F32)

    def finish(part):
        @pl.when(jnp.logical_not(inner_z))
        def _():
            for e in range(experts):
                outward[part, e].wait_recv()
                wg_ref[e, :, part * ff : (part + 1) * ff] = z_fin[part, e].astype(F32)

    def rows_of(member, carry):
        at = columns(member)

        def both(part):
            cols = slice(part * ff, (part + 1) * ff)
            return jnp.concatenate([w_all[member, e, :, cols] for e in range(experts)], axis=1)

        out_ref[:, at] = dot(ops[2], both(2), NT).astype(BF16)
        grad_ref[:, at] = (dot(ops[0], both(0), NT) + dot(ops[1], both(1), NT)).astype(BF16)
        return carry

    begin(0)
    turn(0)
    begin(1)
    enter(0)
    turn(1)
    begin(2)
    meet(0)
    enter(1)
    turn(2)
    leave(0)
    lax.fori_loop(0, INNER // 2, rows_of, 0)
    meet(1)
    leave(1)
    enter(2)
    meet(2)
    lax.fori_loop(INNER // 2, INNER, rows_of, 0)
    leave(2)
    for part in range(parts):
        finish(part)

    @pl.when(inner_z)
    def _():
        for k in pieces:
            across[k].wait_send()
            outward[k].wait_send()

    @pl.when(jnp.logical_not(inner_z))
    def _():
        for k in pieces:
            inward[k].wait_send()

    for copy in [over_x, over_y, on_x, on_y, pair_x, pair_y] + cross:
        copy.wait_send()
    for part in range(parts):
        for copy in first[part] + second[part] + [swap(part, d) for d in range(4)]:
            copy.wait_send()


def local(spread, rows_in, cotangent, expert_counts, weights):
    rows, model = rows_in.shape
    own, experts, width = weights.shape
    ff = width // 3
    feat = own * spread

    def regroup(v, a, b):
        return v if spread == 1 else v.reshape(rows, a, b, own).swapaxes(1, 2).reshape(rows, model)

    w = weights.swapaxes(0, 1)
    if spread > 1:
        peers = [[h * INNER + m for h in range(spread)] for m in range(INNER)]
        w = lax.all_gather(w, "shard", axis=1, tiled=True, axis_index_groups=peers)

    vmem = pl.BlockSpec(memory_space=pltpu.VMEM)
    dma = pltpu.SemaphoreType.DMA
    block = (feat, width)
    rows_out, rows_grad, wg = pl.pallas_call(
        kernel,
        out_shape=(
            jax.ShapeDtypeStruct((rows, model), BF16),
            jax.ShapeDtypeStruct((rows, model), BF16),
            jax.ShapeDtypeStruct((experts, feat, width), F32),
        ),
        in_specs=[
            pl.BlockSpec(memory_space=pltpu.SMEM), vmem, vmem,
            pl.BlockSpec(memory_space=pl.ANY),
        ],
        out_specs=(vmem, vmem, vmem),
        scratch_shapes=[
            pltpu.VMEM((INNER, experts, *block), BF16),
            pltpu.VMEM((rows, 2 * ff), F32),
            pltpu.VMEM((rows, ff), F32),
            pltpu.VMEM((3, rows, experts * ff), BF16),
            pltpu.VMEM((3, 4, feat, experts * ff), BF16),
            pltpu.VMEM((3, 4, feat, experts * ff), BF16),
            pltpu.VMEM((3, 4, feat, ff), BF16),
            pltpu.VMEM((3, 4, feat, ff), BF16),
            pltpu.VMEM((3, 2, feat, ff), BF16),
            pltpu.VMEM((3, 2, feat, ff), BF16),
            pltpu.VMEM((3, 4, feat, ff), F32),
            pltpu.VMEM((3, experts, feat, ff), BF16),
            pltpu.VMEM((3, experts, feat, ff), BF16),
            pltpu.VMEM((3, experts, feat, ff), BF16),
            pltpu.VMEM((3, experts, feat, ff), BF16),
            dma,
            dma((14,)), dma((14,)),
            dma((3, 4)), dma((3, 4)),
            dma((3, 6)), dma((3, 6)),
            dma((3, 3, experts)), dma((3, 3, experts)),
        ],
        compiler_params=pltpu.CompilerParams(
            collective_id=0, has_side_effects=True, vmem_limit_bytes=62 * 1024 * 1024 - 1024 * 1024
        ),
        cost_estimate=pl.CostEstimate(
            flops=12 * rows * model * experts * width // 3 * 3, bytes_accessed=32 << 20,
            transcendentals=rows * ff,
        ),
    )(expert_counts, regroup(rows_in, spread, INNER), regroup(cotangent, spread, INNER), w)
    if spread > 1:
        wg = lax.psum_scatter(
            wg, "shard", scatter_dimension=1, tiled=True, axis_index_groups=peers
        )
    return regroup(rows_out, INNER, spread), regroup(rows_grad, INNER, spread), wg.swapaxes(0, 1)


def solution(mesh):
    rows_spec = P(("shard", "rep"), None)
    weight_spec = P("shard", None, None)
    return jax.shard_map(
        functools.partial(local, mesh.shape["shard"] // INNER),
        mesh=mesh,
        in_specs=(rows_spec, rows_spec, rows_spec, weight_spec),
        out_specs=(rows_spec, rows_spec, weight_spec),
        check_vma=False,
    )
```

```python
import functools

import jax
import jax.numpy as jnp
from jax import lax
from jax.experimental import pallas as pl
from jax.experimental.pallas import tpu as pltpu
from jax.sharding import PartitionSpec as P

BLOCK = 128
INNER = 8
MESH = pl.DeviceIdType.MESH
BF16, F32 = jnp.bfloat16, jnp.float32


def flip(index, bit):
    return index + bit - 2 * bit * lax.rem(lax.div(index, bit), 2)


def dot(a, b, dims):
    return lax.dot_general(a, b, (dims, ((), ())), preferred_element_type=F32)


NN, NT, TN = ((1,), (0,)), ((1,), (1,)), ((0,), (0,))


def kernel(
    counts_ref, x_hbm, dy_hbm, w_ref,
    out_hbm, grad_hbm, wg_ref,
    x_ref, dy_ref, out_ref, grad_ref, w_all, pre, hgrad, ops,
    core_out, core_in, first_out, first_in, second_out, second_in, acc,
    z_out, z_in, z_peer, z_fin,
    w_sem, row_sem, ag_send, ag_recv, core_send, core_recv, xy_send, xy_recv, z_send, z_recv,
):
    rows = x_ref.shape[0]
    experts, feat, width = w_ref.shape
    ff = width // 3
    shard = lax.axis_index("shard")
    rep = lax.axis_index("rep")
    local = lax.rem(shard, INNER)
    to_core, to_x, to_y = ((flip(shard, b), rep) for b in (1, 2, 4))
    z_pair, z_mirror = (shard, flip(rep, 1)), (shard, 3 - rep)
    inner_z = jnp.logical_or(rep == 1, rep == 2)
    partner = flip(local, 1)
    near = [local, flip(local, 2), flip(local, 4), flip(flip(local, 2), 4)]
    far = [partner, flip(partner, 2), flip(partner, 4), flip(flip(partner, 2), 4)]

    load = pltpu.make_async_copy(w_ref, w_all.at[local], w_sem)
    load.start()
    loads = [
        pltpu.make_async_copy(x_hbm, x_ref, row_sem.at[0]),
        pltpu.make_async_copy(dy_hbm, dy_ref, row_sem.at[1]),
    ]
    barrier = pltpu.get_barrier_semaphore()
    for other in (to_core, to_x, to_y, z_pair, z_mirror):
        pl.semaphore_signal(barrier, inc=1, device_id=other, device_id_type=MESH)
    load.wait()
    pl.semaphore_wait(barrier, 5)

    ex = lax.rem(rep, 2)
    ey = 1 - ex

    def share(k, member, e, device):
        block = w_all.at[member, e]
        return pltpu.make_async_remote_copy(
            src_ref=block, dst_ref=block, send_sem=ag_send.at[k], recv_sem=ag_recv.at[k],
            device_id=device, device_id_type=MESH,
        )

    over_x, over_y = share(0, near[0], ex, to_x), share(1, near[0], ey, to_y)
    on_y, on_x = share(2, near[1], ex, to_y), share(3, near[2], ey, to_x)
    pair_x, pair_y = share(4, near[1], ex, z_pair), share(5, near[2], ey, z_pair)
    held = [
        (0, 0), (0, 1), (1, ex), (2, ey), (1, ey), (2, ex), (3, ex), (3, ey),
    ]
    cross = [share(6 + k, near[d], e, to_core) for k, (d, e) in enumerate(held)]
    over_x.start()
    over_y.start()
    cross[0].start()
    cross[1].start()
    for copy in loads:
        copy.start()

    def span(e):
        padded = lax.div(counts_ref[0, 0] + (BLOCK - 1), BLOCK) * BLOCK
        begin = e * padded
        return begin, begin + counts_ref[0, e]

    def columns(member):
        return pl.ds(pl.multiple_of(member * feat, 128), feat)

    def project(member, e, first=False):
        position = lax.broadcasted_iota(jnp.int32, (rows, 1), 0)
        begin, end = span(e)
        keep = (position >= begin) & (position < end)
        x = x_ref[:, columns(member)]
        dy = dy_ref[:, columns(member)]
        zero = jnp.zeros_like(x)
        p = dot(jnp.where(keep, x, zero), w_all[member, e, :, : 2 * ff], NN)
        h = dot(jnp.where(keep, dy, zero), w_all[member, e, :, 2 * ff :], NN)
        if first:
            pre[...] = p
            hgrad[...] = h
        else:
            pre[...] += p
            hgrad[...] += h

    for copy in loads:
        copy.wait()
    project(near[0], 0, True)
    project(near[0], 1)
    cross[0].wait_recv()
    cross[1].wait_recv()
    project(far[0], 0)
    project(far[0], 1)
    over_x.wait_recv()
    on_y.start()
    pair_x.start()
    cross[2].start()
    over_y.wait_recv()
    on_x.start()
    pair_y.start()
    cross[3].start()
    project(near[1], ex)
    project(near[2], ey)
    cross[2].wait_recv()
    project(far[1], ex)
    cross[3].wait_recv()
    project(far[2], ey)
    for k, copy in ((4, pair_x), (5, pair_y), (6, on_y), (7, on_x)):
        copy.wait_recv()
        cross[k].start()
    for d, e in held[4:]:
        project(near[d], e)
    for k in range(4, 8):
        cross[k].wait_recv()
        project(far[held[k][0]], held[k][1])

    def activate(i, carry):
        at = pl.ds(pl.multiple_of(i * BLOCK, BLOCK), BLOCK)
        a, b, g = pre[at, :ff], pre[at, ff:], hgrad[at, :]
        s = jax.nn.sigmoid(a)
        active = a * s
        values = (
            (g * b * s * (1.0 + a * (1.0 - s))).astype(BF16),
            (g * active).astype(BF16),
            (active * b).astype(BF16),
        )
        place = lax.broadcasted_iota(jnp.int32, (BLOCK, 1), 0) + i * BLOCK
        for e in range(experts):
            begin, end = span(e)
            keep = (place >= begin) & (place < end)
            for part, value in enumerate(values):
                ops[part, at, e * ff : (e + 1) * ff] = jnp.where(
                    keep, value, jnp.zeros_like(value)
                )
        return carry

    lax.fori_loop(0, rows // BLOCK, activate, 0)

    parts = 3

    def terms(member, part):
        source = dy_ref if part == 2 else x_ref
        return dot(source[:, columns(member)], ops[part], TN)

    def swap(part, d):
        return pltpu.make_async_remote_copy(
            src_ref=core_out.at[part, d], dst_ref=core_in.at[part, d],
            send_sem=core_send.at[part, d], recv_sem=core_recv.at[part, d],
            device_id=to_core, device_id_type=MESH,
        )

    def to_partner(part, d):
        core_out[part, d] = terms(far[d], part).astype(BF16)
        swap(part, d).start()

    def own_terms(part, d):
        value = terms(near[d], part)
        swap(part, d).wait_recv()
        value = value + core_in[part, d].astype(F32)
        return value[:, :ff], value[:, ff:]

    def step(part, k, src, dst, device):
        return pltpu.make_async_remote_copy(
            src_ref=src, dst_ref=dst, send_sem=xy_send.at[part, k], recv_sem=xy_recv.at[part, k],
            device_id=device, device_id_type=MESH,
        )

    first = [
        [step(p, k, first_out.at[p, k], first_in.at[p, k], (to_x, to_y)[k % 2]) for k in range(4)]
        for p in range(parts)
    ]
    second = [
        [step(p, 4 + k, second_out.at[p, k], second_in.at[p, k], (to_y, to_x)[k]) for k in range(2)]
        for p in range(parts)
    ]

    def send_first(part, k, value):
        first_out[part, k] = value.astype(BF16)
        first[part][k].start()

    def begin(part):
        to_partner(part, 3)
        to_partner(part, 1)
        zero, one = own_terms(part, 3)
        send_first(part, 0, zero)
        send_first(part, 1, one)
        to_partner(part, 2)
        zero, one = own_terms(part, 1)
        send_first(part, 2, zero)
        acc[part, 1] = one
        to_partner(part, 0)
        zero, one = own_terms(part, 2)
        send_first(part, 3, one)
        acc[part, 0] = zero
        zero, one = own_terms(part, 0)
        acc[part, 2] = zero
        acc[part, 3] = one

    def turn(part):
        for k in range(2):
            first[part][k].wait_recv()
            second_out[part, k] = (acc[part, k] + first_in[part, k].astype(F32)).astype(BF16)
            second[part][k].start()

    def hop(j, part, e, src, dst, device):
        return pltpu.make_async_remote_copy(
            src_ref=src.at[part, e], dst_ref=dst.at[part, e],
            send_sem=z_send.at[j, part, e], recv_sem=z_recv.at[j, part, e],
            device_id=device, device_id_type=MESH,
        )

    pieces = [(p, e) for p in range(parts) for e in range(experts)]
    inward = {k: hop(0, *k, z_out, z_in, z_pair) for k in pieces}
    across = {k: hop(1, *k, z_out, z_peer, z_mirror) for k in pieces}
    outward = {k: hop(2, *k, z_fin, z_fin, z_pair) for k in pieces}

    def enter(part):
        for e in range(experts):
            first[part][2 + e].wait_recv()
            second[part][e].wait_recv()
            total = (
                acc[part, 2 + e]
                + first_in[part, 2 + e].astype(F32)
                + second_in[part, e].astype(F32)
            )

            @pl.when(jnp.logical_not(inner_z))
            def _():
                z_out[part, e] = total.astype(BF16)
                inward[part, e].start()

            @pl.when(inner_z)
            def _():
                acc[part, 2 + e] = total

    def meet(part):
        @pl.when(inner_z)
        def _():
            for e in range(experts):
                inward[part, e].wait_recv()
                z_out[part, e] = (acc[part, 2 + e] + z_in[part, e].astype(F32)).astype(BF16)
                across[part, e].start()

    def leave(part):
        @pl.when(inner_z)
        def _():
            for e in range(experts):
                across[part, e].wait_recv()
                z_fin[part, e] = (
                    z_out[part, e].astype(F32) + z_peer[part, e].astype(F32)
                ).astype(BF16)
                outward[part, e].start()
                wg_ref[e, :, part * ff : (part + 1) * ff] = z_fin[part, e]

    def finish(part):
        @pl.when(jnp.logical_not(inner_z))
        def _():
            for e in range(experts):
                outward[part, e].wait_recv()
                wg_ref[e, :, part * ff : (part + 1) * ff] = z_fin[part, e]

    def rows_of(member, carry):
        at = columns(member)

        def both(part):
            cols = slice(part * ff, (part + 1) * ff)
            return jnp.concatenate([w_all[member, e, :, cols] for e in range(experts)], axis=1)

        out_ref[:, at] = dot(ops[2], both(2), NT).astype(BF16)
        grad_ref[:, at] = (dot(ops[0], both(0), NT) + dot(ops[1], both(1), NT)).astype(BF16)
        return carry

    begin(0)
    turn(0)
    begin(1)
    enter(0)
    turn(1)
    begin(2)
    meet(0)
    enter(1)
    turn(2)
    leave(0)
    lax.fori_loop(0, INNER // 2, rows_of, 0)
    meet(1)
    leave(1)
    enter(2)
    meet(2)
    lax.fori_loop(INNER // 2, INNER, rows_of, 0)
    stores = [
        pltpu.make_async_copy(out_ref, out_hbm, row_sem.at[2]),
        pltpu.make_async_copy(grad_ref, grad_hbm, row_sem.at[3]),
    ]
    for copy in stores:
        copy.start()
    leave(2)
    for part in range(parts):
        finish(part)

    @pl.when(inner_z)
    def _():
        for k in pieces:
            across[k].wait_send()
            outward[k].wait_send()

    @pl.when(jnp.logical_not(inner_z))
    def _():
        for k in pieces:
            inward[k].wait_send()

    for copy in stores:
        copy.wait()
    for copy in [over_x, over_y, on_x, on_y, pair_x, pair_y] + cross:
        copy.wait_send()
    for part in range(parts):
        for copy in first[part] + second[part] + [swap(part, d) for d in range(4)]:
            copy.wait_send()


def local(spread, rows_in, cotangent, expert_counts, weights):
    rows, model = rows_in.shape
    own, experts, width = weights.shape
    ff = width // 3
    feat = own * spread

    def regroup(v, a, b):
        return v if spread == 1 else v.reshape(rows, a, b, own).swapaxes(1, 2).reshape(rows, model)

    w = weights.swapaxes(0, 1)
    if spread > 1:
        peers = [[h * INNER + m for h in range(spread)] for m in range(INNER)]
        w = lax.all_gather(w, "shard", axis=1, tiled=True, axis_index_groups=peers)

    vmem = pl.BlockSpec(memory_space=pltpu.VMEM)
    hbm = pl.BlockSpec(memory_space=pl.ANY)
    dma = pltpu.SemaphoreType.DMA
    block = (feat, width)
    rows_out, rows_grad, wg = pl.pallas_call(
        kernel,
        out_shape=(
            jax.ShapeDtypeStruct((rows, model), BF16),
            jax.ShapeDtypeStruct((rows, model), BF16),
            jax.ShapeDtypeStruct((experts, feat, width), BF16),
        ),
        in_specs=[
            pl.BlockSpec(memory_space=pltpu.SMEM), hbm, hbm, hbm,
        ],
        out_specs=(hbm, hbm, vmem),
        scratch_shapes=[pltpu.VMEM((rows, model), BF16)] * 4 + [
            pltpu.VMEM((INNER, experts, *block), BF16),
            pltpu.VMEM((rows, 2 * ff), F32),
            pltpu.VMEM((rows, ff), F32),
            pltpu.VMEM((3, rows, experts * ff), BF16),
            pltpu.VMEM((3, 4, feat, experts * ff), BF16),
            pltpu.VMEM((3, 4, feat, experts * ff), BF16),
            pltpu.VMEM((3, 4, feat, ff), BF16),
            pltpu.VMEM((3, 4, feat, ff), BF16),
            pltpu.VMEM((3, 2, feat, ff), BF16),
            pltpu.VMEM((3, 2, feat, ff), BF16),
            pltpu.VMEM((3, 4, feat, ff), F32),
            pltpu.VMEM((3, experts, feat, ff), BF16),
            pltpu.VMEM((3, experts, feat, ff), BF16),
            pltpu.VMEM((3, experts, feat, ff), BF16),
            pltpu.VMEM((3, experts, feat, ff), BF16),
            dma,
            dma((4,)),
            dma((14,)), dma((14,)),
            dma((3, 4)), dma((3, 4)),
            dma((3, 6)), dma((3, 6)),
            dma((3, 3, experts)), dma((3, 3, experts)),
        ],
        compiler_params=pltpu.CompilerParams(
            collective_id=0, has_side_effects=True, vmem_limit_bytes=62 * 1024 * 1024 - 1024 * 1024
        ),
        cost_estimate=pl.CostEstimate(
            flops=12 * rows * model * experts * width // 3 * 3, bytes_accessed=32 << 20,
            transcendentals=rows * ff,
        ),
    )(expert_counts, regroup(rows_in, spread, INNER), regroup(cotangent, spread, INNER), w)
    wg = wg.astype(F32)
    if spread > 1:
        wg = lax.psum_scatter(
            wg, "shard", scatter_dimension=1, tiled=True, axis_index_groups=peers
        )
    return regroup(rows_out, INNER, spread), regroup(rows_grad, INNER, spread), wg.swapaxes(0, 1)


def solution(mesh):
    rows_spec = P(("shard", "rep"), None)
    weight_spec = P("shard", None, None)
    return jax.shard_map(
        functools.partial(local, mesh.shape["shard"] // INNER),
        mesh=mesh,
        in_specs=(rows_spec, rows_spec, rows_spec, weight_spec),
        out_specs=(rows_spec, rows_spec, weight_spec),
        check_vma=False,
    )
```
